32 devices in a mesh: rad: 4 (over y, core), mode: 8 (over z, x).
Axes of the slice: x: 2, y: 2, z: 4, core: 2. Of those that a mesh axis runs over, the one named last changes fastest.
Arguments:
- spectra: bfloat16 [2, 128, 1024, 1024], P(None, 'mode', 'rad'), may hold values from -6 to 6
- diffusivity: float32 [1024], replicated, may hold values from 0.1 to 1
- eigenvalues: float32 [1024], replicated, may hold values from 0.3 to 3
- radial_basis: bfloat16 [1024, 1024], replicated, may hold values from -0.1875 to 0.1875
- dual_basis: bfloat16 [1024, 1024], replicated, may hold values from -0.1875 to 0.1875
- degree_count: int32 [128], replicated, may hold values from 1 to 1024, as said below
- order_slot: int32 [128], replicated, may hold values from 0 to 127, as said below
Outputs:
- stepped: bfloat16 [2, 128, 1024, 1024], P(None, 'mode', 'rad')
The draws below stay inside these ranges and needn't reach their ends.
Inputs may be any that keep to these rules, and one draw needn't show every extreme that they name: `degree_count`: row i holds order m_i = floor(i * 4); at most 1024 - m_i of its slots are live, and row 0 has all 1024. `order_slot`: A permutation of the rows. Output row d * 16 + s * 2 + k takes an input row of block s, that is one of s * 16 to (s + 1) * 16 - 1.
All inputs are finite; a program needn't handle non-finite values.
Results may differ from the reference program's by a relative error of at most 0.0065.
Values may be sent and summed in bfloat16 or wider, within the bound.
A program may use at most 192 MiB of HBM per device.

```python
import math
import jax
import jax.numpy as jnp
from jax import lax

NR = 1024
L = 1024
ORD_DEV = 16
NM = 128
SHARE = 2
N_MODE = 8


def draw_degree_count(key, part):
    row_ids = jnp.arange(NM, dtype=jnp.int32)
    orders = row_ids * L // (2 * NM)
    trimmed = jax.random.randint(key, (NM,), 0, L // 16, dtype=jnp.int32)
    trimmed = jnp.where(row_ids == 0, 0, trimmed)
    return (L - orders - trimmed).astype(jnp.int32)


def draw_order_slot(key, part):
    source_keys = jax.random.split(jax.random.fold_in(key, 7), N_MODE)
    orderings = jax.vmap(lambda sub_key: jax.random.permutation(sub_key, ORD_DEV))(source_keys)
    orderings = orderings.astype(jnp.int32).reshape(N_MODE, N_MODE, SHARE)
    offsets = (jnp.arange(N_MODE, dtype=jnp.int32) * ORD_DEV)[:, None, None]
    chosen = orderings + offsets
    return jnp.transpose(chosen, (1, 0, 2)).reshape(NM).astype(jnp.int32)


def levels(key, shape, pieces, least, high):
    def one(dim, parts):
        steps = jax.random.uniform(jax.random.fold_in(jax.random.fold_in(key, 6), dim), (parts,), jnp.float32, least / len(pieces), high / len(pieces))
        return jnp.repeat(jnp.exp(steps), shape[dim] // parts).reshape((-1,) + (1,) * (len(shape) - dim - 1))

    gain = one(*pieces[0])
    for cut in pieces[1:]:
        gain = gain * one(*cut)
    return gain


def gaussian(own_key, extent, deviation, most, cuts=(), kind=jnp.bfloat16):
    loudness = levels(own_key, extent, cuts, -0.22, 0.18) if cuts else 1.0
    result = jax.random.normal(own_key, extent, jnp.float32) * deviation * loudness
    return jnp.minimum(jnp.maximum(result, -most), most).astype(kind)


def setup_inputs(seed: int = 0) -> dict:
    arg_keys = jax.random.split(jax.random.key(seed), 8)
    spectra = gaussian(arg_keys[0], (2, NM, NR, L), 1.0, 6.0, ((1, 8), (2, 4)))
    diffusivity = jnp.clip(jnp.exp(jax.random.uniform(arg_keys[1], (NR,), jnp.float32, math.log(0.1), math.log(1.0))), 0.1, 1.0)
    eigenvalues = jnp.clip(jnp.exp(jax.random.uniform(arg_keys[2], (NR,), jnp.float32, math.log(0.3), math.log(3.0))), 0.3, 3.0)
    radial_basis = gaussian(arg_keys[3], (NR, NR), NR ** -0.5, 0.1875)
    dual_basis = gaussian(arg_keys[4], (NR, NR), NR ** -0.5, 0.1875)
    degree_count = draw_degree_count(jax.random.fold_in(arg_keys[7], 71), 0)
    order_slot = draw_order_slot(jax.random.fold_in(arg_keys[7], 71), 0)
    return {"spectra": spectra, "diffusivity": diffusivity, "eigenvalues": eigenvalues, "radial_basis": radial_basis, "dual_basis": dual_basis, "degree_count": degree_count, "order_slot": order_slot}


def degree_table(counts, order_start, order_rows, slot_start, slot_width, slots_total, orders_total):
    row_ids = order_start + jnp.arange(order_rows, dtype=jnp.int32)
    orders = (row_ids * slots_total) // (2 * orders_total)
    slot_ids = slot_start + jnp.arange(slot_width, dtype=jnp.int32)
    degree = (orders[:, None] + slot_ids[None, :]).astype(jnp.float32)
    limits = lax.dynamic_slice_in_dim(counts, order_start, order_rows)
    live_mask = slot_ids[None, :] < limits[:, None]
    return degree, live_mask


def explicit(padded, kappa_rows, radius_start, degree, live_mask, shells_total):
    center = padded[:, :, 2:-2]
    shell_rows = center.shape[2]
    second = (-padded[:, :, :-4] + 16.0 * padded[:, :, 1:-3] - 30.0 * center
              + 16.0 * padded[:, :, 3:-1] - padded[:, :, 4:]) / 12.0
    radius = 1.2 + (radius_start + jnp.arange(shell_rows, dtype=jnp.int32)).astype(jnp.float32) / shells_total
    damping = (degree * (degree + 1.0))[None, :, None, :] / ((shells_total * radius) ** 2)[None, None, :, None]
    updated = center + 0.5 * kappa_rows[None, None, :, None] * (second - damping * center)
    return jnp.where(live_mask[None, :, None, :], updated, 0.0).astype(jnp.bfloat16)


def reference(spectra, diffusivity, eigenvalues, radial_basis, dual_basis, degree_count, order_slot):
    orders_total = spectra.shape[1]
    shells_total = spectra.shape[2]
    slots_total = spectra.shape[3]
    block = math.gcd(orders_total, 16)
    identity = jnp.eye(shells_total, dtype=jnp.float32)
    basis_full = (identity + radial_basis.astype(jnp.float32)).astype(jnp.bfloat16)
    dual_full = (identity + dual_basis.astype(jnp.float32)).astype(jnp.bfloat16)
    basis_full = lax.optimization_barrier(basis_full).astype(jnp.float32)
    dual_full = lax.optimization_barrier(dual_full).astype(jnp.float32)

    def one_block(block_index):
        start = (block_index * block).astype(jnp.int32)
        piece = lax.dynamic_slice_in_dim(spectra, start, block, 1).astype(jnp.float32)
        degree, live_mask = degree_table(degree_count, start, block, 0, slots_total, slots_total, orders_total)
        padded = jnp.pad(piece, ((0, 0), (0, 0), (2, 2), (0, 0)))
        updated = explicit(padded, diffusivity, 0, degree, live_mask, shells_total)
        updated = lax.optimization_barrier(updated).astype(jnp.float32)
        projected = jnp.einsum('kr,cirj->cikj', dual_full, updated)
        divisor = eigenvalues[None, None, :, None] + 0.5 * (degree * (degree + 1.0))[None, :, None, :] / (shells_total * shells_total)
        scaled = (projected / divisor).astype(jnp.bfloat16)
        scaled = lax.optimization_barrier(scaled).astype(jnp.float32)
        restored = jnp.einsum('kr,cirj->cikj', basis_full, scaled)
        return jnp.where(live_mask[None, :, None, :], restored, 0.0).astype(jnp.bfloat16)

    stacked = lax.map(one_block, jnp.arange(orders_total // block, dtype=jnp.int32))
    solved = jnp.moveaxis(stacked, 0, 1).reshape(2, orders_total, shells_total, slots_total)
    return jnp.take(solved, order_slot, axis=1)
```

```python
import functools

import jax
import jax.numpy as jnp
from jax import lax
from jax.experimental import pallas as pl
from jax.experimental.pallas import tpu as pltpu
from jax.sharding import PartitionSpec as P

SPLIT = 2
AHEAD = 2
SEND_SLOTS = 3
OUT_SLOTS = 4
PAD = 16
TILE = 256
ROWS = 128


def kernel(
    sizes,
    order_ref,
    count_ref,
    spectra_ref,
    kappa_ref,
    eigen_ref,
    basis_ref,
    dual_ref,
    out_ref,
    spec,
    basis,
    dual,
    recv,
    send,
    upd,
    obuf,
    load_sem,
    send_sem,
    recv_sem,
    osend_sem,
    orecv_sem,
):
    parts, modes, rows, shells, slots, orders = sizes
    block = shells // parts
    per = rows // modes
    width = slots // SPLIT
    pairs = 2 * rows // parts
    steps = pairs * SPLIT
    q = lax.axis_index("rad")
    s = lax.axis_index("mode")

    load = pltpu.make_async_copy(spectra_ref, spec, load_sem.at[0])
    load.start()
    load_basis = pltpu.make_async_copy(basis_ref, basis, load_sem.at[1])
    load_basis.start()
    load_dual = pltpu.make_async_copy(dual_ref, dual, load_sem.at[2])
    load_dual.start()

    barrier = pltpu.get_barrier_semaphore()
    count = parts * modes
    me = q * modes + s

    def greet(i, _):
        other = lax.rem(me + i, count)
        pl.semaphore_signal(
            barrier,
            inc=1,
            device_id={"rad": other // modes, "mode": lax.rem(other, modes)},
            device_id_type=pl.DeviceIdType.MESH,
        )
        return 0

    lax.fori_loop(1, count, greet, 0)

    def pair(who, step):
        half = lax.rem(who, 2)
        turn = lax.rem(step // SPLIT + (s * pairs) // modes + 2 * who, pairs)
        p = 2 * turn + half
        return who // 2, p // per, lax.rem(p, per), lax.rem(step, SPLIT)

    def shell_copy(who, step):
        slot = lax.rem(step, SEND_SLOTS)
        return pltpu.make_async_remote_copy(
            src_ref=send.at[slot, who],
            dst_ref=recv.at[step, pl.ds(PAD + q * block, block)],
            send_sem=send_sem.at[slot, who],
            recv_sem=recv_sem.at[step, q],
            device_id={"rad": who, "mode": s},
            device_id_type=pl.DeviceIdType.MESH,
        )

    def read_row(who, step):
        c, d, k, piece = pair(who, step)
        row = lax.rem(order_ref[d * rows + s * per + k], rows)
        cols = pl.ds(pl.multiple_of(piece * width, width), width)
        return spec[c, row, :, cols]

    def push(step):
        slot = lax.rem(step, SEND_SLOTS)

        def one(i, _):
            who = lax.rem(q + i, parts)

            @pl.when(step >= SEND_SLOTS)
            def _():
                shell_copy(who, step - SEND_SLOTS).wait_send()

            send[slot, who] = read_row(who, step)
            shell_copy(who, step).start()
            return 0

        lax.fori_loop(1, parts, one, 0)
        recv[step, pl.ds(PAD + q * block, block), :] = read_row(q, step)

    def arrive(step):
        def one(i, _):
            who = lax.rem(q + i, parts)
            pltpu.make_async_remote_copy(
                src_ref=send.at[0, who],
                dst_ref=recv.at[step, pl.ds(PAD + who * block, block)],
                send_sem=send_sem.at[0, who],
                recv_sem=recv_sem.at[step, who],
                device_id={"rad": who, "mode": s},
                device_id_type=pl.DeviceIdType.MESH,
            ).wait_recv()
            return 0

        lax.fori_loop(1, parts, one, 0)

    def result_copies(step, act_remote, act_local):
        c, d, k, piece = pair(q, step)
        slot = lax.rem(step, OUT_SLOTS)
        cols = pl.ds(pl.multiple_of(piece * width, width), width)

        def one(i, _):
            who = lax.rem(q + i, parts)
            src = obuf.at[slot, pl.ds(who * block, block)]
            dst = out_ref.at[c, s * per + k, :, cols]
            here = (d == s) & (who == q)

            @pl.when(here)
            def _():
                act_local(pltpu.make_async_copy(src, dst, osend_sem.at[slot, who]))

            @pl.when(jnp.logical_not(here))
            def _():
                act_remote(
                    pltpu.make_async_remote_copy(
                        src_ref=src,
                        dst_ref=dst,
                        send_sem=osend_sem.at[slot, who],
                        recv_sem=orecv_sem.at[c, s * per + k],
                        device_id={"rad": who, "mode": d},
                        device_id_type=pl.DeviceIdType.MESH,
                    )
                )

            return 0

        lax.fori_loop(0, parts, one, 0)

    zero_pad = jnp.zeros((PAD, width), jnp.bfloat16)

    def clear(step, _):
        recv[step, pl.ds(0, PAD), :] = zero_pad
        recv[step, pl.ds(PAD + shells, PAD), :] = zero_pad
        return 0

    lax.fori_loop(0, steps, clear, 0)
    load.wait()
    pl.semaphore_wait(barrier, count - 1)
    for first in range(AHEAD):
        push(jnp.int32(first))

    load_basis.wait()
    load_dual.wait()

    def add_identity(i, _):
        at = pl.ds(pl.multiple_of(i * ROWS, ROWS), ROWS)
        row = lax.broadcasted_iota(jnp.int32, (ROWS, shells), 0) + i * ROWS
        col = lax.broadcasted_iota(jnp.int32, (ROWS, shells), 1)
        eye = jnp.where(row == col, 1.0, 0.0).astype(jnp.float32)
        basis[at, :] = (eye + basis[at, :].astype(jnp.float32)).astype(jnp.bfloat16)
        dual[at, :] = (eye + dual[at, :].astype(jnp.float32)).astype(jnp.bfloat16)
        return 0

    lax.fori_loop(0, shells // ROWS, add_identity, 0)

    def body(step, _):
        @pl.when(step + AHEAD < steps)
        def _():
            push(step + AHEAD)

        arrive(step)
        c, d, k, piece = pair(q, step)
        row_id = order_ref[d * rows + s * per + k]
        limit = count_ref[row_id]
        order = (row_id * slots) // (2 * orders)
        slot = lax.rem(step, OUT_SLOTS)

        def table(ct):
            ids = (
                lax.broadcasted_iota(jnp.int32, (1, TILE), 1) + piece * width + ct * TILE
            )
            degree = (order + ids).astype(jnp.float32)
            return degree * (degree + 1.0), ids < limit

        def stencil(i, _):
            ct = lax.rem(i, width // TILE)
            rb = i // (width // TILE)
            at = pl.multiple_of(rb * ROWS, ROWS)
            cols = pl.ds(pl.multiple_of(ct * TILE, TILE), TILE)
            ext = recv[step, pl.ds(at, ROWS + 2 * PAD), cols].astype(jnp.float32)
            size = ROWS + 2 * PAD

            def near(o):
                return pltpu.roll(ext, (size - o) % size, 0)[PAD : PAD + ROWS]

            f = ext[PAD : PAD + ROWS]
            second = (
                16.0 * (near(-1) + near(1)) - (near(-2) + near(2)) - 30.0 * f
            ) * (1.0 / 12.0)
            ll, live = table(ct)
            shell = lax.broadcasted_iota(jnp.int32, (ROWS, 1), 0) + at
            rho = 1.2 + shell.astype(jnp.float32) / shells
            inverse = 1.0 / ((shells * rho) * (shells * rho))
            half = 0.5 * kappa_ref[pl.ds(at, ROWS), :]
            value = f + half * (second - (ll * inverse) * f)
            value = jnp.where(live, value, 0.0)
            upd[pl.ds(at, ROWS), cols] = value.astype(jnp.bfloat16)
            return 0

        lax.fori_loop(0, (shells // ROWS) * (width // TILE), stencil, 0)

        @pl.when(step >= OUT_SLOTS)
        def _():
            result_copies(
                step - OUT_SLOTS, lambda r: r.wait_send(), lambda l: l.wait()
            )

        def transform(ct, _):
            cols = pl.ds(pl.multiple_of(ct * TILE, TILE), TILE)
            ll, live = table(ct)
            projected = jnp.dot(
                dual[...], upd[:, cols], preferred_element_type=jnp.float32
            )
            divisor = eigen_ref[...] + ll * (0.5 / (slots * slots))
            scaled = (projected / divisor).astype(jnp.bfloat16)
            restored = jnp.dot(basis[...], scaled, preferred_element_type=jnp.float32)
            obuf[slot, :, cols] = jnp.where(live, restored, 0.0).astype(jnp.bfloat16)
            return 0

        lax.fori_loop(0, width // TILE, transform, 0)
        result_copies(step, lambda r: r.start(), lambda l: l.start())
        return 0

    lax.fori_loop(0, steps, body, 0)

    def drain_send(i, _):
        step = steps - SEND_SLOTS + i // (parts - 1)
        who = lax.rem(q + 1 + lax.rem(i, parts - 1), parts)
        shell_copy(who, step).wait_send()
        return 0

    lax.fori_loop(0, SEND_SLOTS * (parts - 1), drain_send, 0)

    def drain_out(i, _):
        result_copies(
            steps - OUT_SLOTS + i, lambda r: r.wait_send(), lambda l: l.wait()
        )
        return 0

    lax.fori_loop(0, OUT_SLOTS, drain_out, 0)

    def landed(i, _):
        c = i // rows
        row = lax.rem(i, rows)
        source = row // per
        p = s * per + lax.rem(row, per)
        who = 2 * c + lax.rem(p, 2)

        @pl.when(jnp.logical_not((source == s) & (who == q)))
        def _():
            pltpu.make_async_remote_copy(
                src_ref=out_ref.at[c, row],
                dst_ref=out_ref.at[c, row],
                send_sem=osend_sem.at[0, 0],
                recv_sem=orecv_sem.at[c, row],
                device_id={"rad": who, "mode": source},
                device_id_type=pl.DeviceIdType.MESH,
            ).wait_recv()

        return 0

    lax.fori_loop(0, 2 * rows, landed, 0)


def on_device(
    spectra, diffusivity, eigenvalues, radial_basis, dual_basis, degree_count, order_slot
):
    _, rows, block, slots = spectra.shape
    shells = diffusivity.shape[0]
    orders = degree_count.shape[0]
    parts = lax.axis_size("rad")
    modes = lax.axis_size("mode")
    steps = 2 * rows // parts * SPLIT
    width = slots // SPLIT
    bf16 = jnp.bfloat16
    dma = pltpu.SemaphoreType.DMA
    sizes = (parts, modes, rows, shells, slots, orders)
    vmem = pl.BlockSpec(memory_space=pltpu.VMEM)
    smem = pl.BlockSpec(memory_space=pltpu.SMEM)
    hbm = pl.BlockSpec(memory_space=pl.ANY)
    return pl.pallas_call(
        functools.partial(kernel, sizes),
        out_shape=jax.ShapeDtypeStruct(spectra.shape, bf16),
        in_specs=[smem, smem, hbm, vmem, vmem, hbm, hbm],
        out_specs=hbm,
        scratch_shapes=[
            pltpu.VMEM(spectra.shape, bf16),
            pltpu.VMEM((shells, shells), bf16),
            pltpu.VMEM((shells, shells), bf16),
            pltpu.VMEM((steps, shells + 2 * PAD, width), bf16),
            pltpu.VMEM((SEND_SLOTS, parts, block, width), bf16),
            pltpu.VMEM((shells, width), bf16),
            pltpu.VMEM((OUT_SLOTS, shells, width), bf16),
            dma((3,)),
            dma((SEND_SLOTS, parts)),
            dma((steps, parts)),
            dma((OUT_SLOTS, parts)),
            dma((2, rows)),
        ],
        compiler_params=pltpu.CompilerParams(
            collective_id=0,
            has_side_effects=True,
            vmem_limit_bytes=60 * 1024 * 1024,
        ),
    )(
        order_slot,
        degree_count,
        spectra,
        diffusivity.reshape(shells, 1),
        eigenvalues.reshape(shells, 1),
        radial_basis,
        dual_basis,
    )


def solution(mesh):
    placed = (P(None, "mode", "rad", None), P(), P(), P(), P(), P(), P())
    return jax.shard_map(
        on_device,
        mesh=mesh,
        in_specs=placed,
        out_specs=P(None, "mode", "rad", None),
        check_vma=False,
    )
```

```python
import functools

import jax
import jax.numpy as jnp
from jax import lax
from jax.experimental import pallas as pl
from jax.experimental.pallas import tpu as pltpu
from jax.sharding import PartitionSpec as P

LANES = 128
SPLIT = 2
AHEAD = 2
SEND_SLOTS = 3
OUT_SLOTS = 4
PAD = 16
TILE = 256
ROWS = 128


def kernel(
    sizes,
    order_ref,
    count_ref,
    spectra_ref,
    kappa_ref,
    eigen_ref,
    basis_ref,
    dual_ref,
    out_ref,
    spec,
    basis,
    dual,
    recv,
    send,
    upd,
    obuf,
    zeros,
    load_sem,
    send_sem,
    recv_sem,
    osend_sem,
    orecv_sem,
    fill_sem,
):
    parts, modes, rows, shells, slots, orders = sizes
    block = shells // parts
    per = rows // modes
    width = slots // SPLIT
    pairs = 2 * rows // parts
    steps = pairs * SPLIT
    q = lax.axis_index("rad")
    s = lax.axis_index("mode")

    def live_width(group):
        most = slots - (group * rows * slots) // (2 * orders)
        return (most + LANES - 1) // LANES * LANES

    least = slots - ((modes - 1) * rows * slots) // (2 * orders)
    least = (least + LANES - 1) // LANES * LANES
    wholes = range(least, slots + 1, LANES)
    widths = sorted({min(max(w - i * width, 0), width) for w in wholes for i in range(SPLIT)})

    def sized(value, choices, act):
        for choice in choices:
            if choice:
                pl.when(value == choice)(functools.partial(act, choice))

    def piece_width(group, piece):
        return jnp.clip(live_width(group) - piece * width, 0, width)

    load = pltpu.make_async_copy(spectra_ref, spec, load_sem.at[0])
    load.start()
    load_basis = pltpu.make_async_copy(basis_ref, basis, load_sem.at[1])
    load_basis.start()
    load_dual = pltpu.make_async_copy(dual_ref, dual, load_sem.at[2])
    load_dual.start()

    barrier = pltpu.get_barrier_semaphore()
    count = parts * modes
    me = q * modes + s

    def greet(i, _):
        other = lax.rem(me + i, count)
        pl.semaphore_signal(
            barrier,
            inc=1,
            device_id={"rad": other // modes, "mode": lax.rem(other, modes)},
            device_id_type=pl.DeviceIdType.MESH,
        )
        return 0

    lax.fori_loop(1, count, greet, 0)

    def pair(who, step):
        half = lax.rem(who, 2)
        turn = lax.rem(step // SPLIT + (s * pairs) // modes + 2 * who, pairs)
        p = 2 * turn + half
        return who // 2, p // per, lax.rem(p, per), lax.rem(step, SPLIT)

    def shell_copy(who, step, act):
        sized(
            piece_width(s, lax.rem(step, SPLIT)),
            widths,
            lambda w: act(shell_copy_of(who, step, w)),
        )

    def shell_copy_of(who, step, w):
        slot = lax.rem(step, SEND_SLOTS)
        return pltpu.make_async_remote_copy(
            src_ref=send.at[slot, who, :, pl.ds(0, w)],
            dst_ref=recv.at[step, pl.ds(PAD + q * block, block), pl.ds(0, w)],
            send_sem=send_sem.at[slot, who],
            recv_sem=recv_sem.at[step, q],
            device_id={"rad": who, "mode": s},
            device_id_type=pl.DeviceIdType.MESH,
        )

    def read_row(who, step):
        c, d, k, piece = pair(who, step)
        row = lax.rem(order_ref[d * rows + s * per + k], rows)
        cols = pl.ds(pl.multiple_of(piece * width, width), width)
        return spec[c, row, :, cols]

    def push(step):
        slot = lax.rem(step, SEND_SLOTS)

        def one(i, _):
            who = lax.rem(q + i, parts)

            @pl.when(step >= SEND_SLOTS)
            def _():
                shell_copy(who, step - SEND_SLOTS, lambda r: r.wait_send())

            send[slot, who] = read_row(who, step)
            shell_copy(who, step, lambda r: r.start())
            return 0

        lax.fori_loop(1, parts, one, 0)

        def keep(w):
            c, d, k, piece = pair(q, step)
            row = lax.rem(order_ref[d * rows + s * per + k], rows)
            cols = pl.ds(pl.multiple_of(piece * width, width), w)
            recv[step, pl.ds(PAD + q * block, block), pl.ds(0, w)] = spec[c, row, :, cols]

        sized(piece_width(s, lax.rem(step, SPLIT)), widths, keep)

    def arrive(step):
        def one(i, _):
            who = lax.rem(q + i, parts)


            def wait(w):
                pltpu.make_async_remote_copy(
                    src_ref=send.at[0, who, :, pl.ds(0, w)],
                    dst_ref=recv.at[
                        step, pl.ds(PAD + who * block, block), pl.ds(0, w)
                    ],
                    send_sem=send_sem.at[0, who],
                    recv_sem=recv_sem.at[step, who],
                    device_id={"rad": who, "mode": s},
                    device_id_type=pl.DeviceIdType.MESH,
                ).wait_recv()

            sized(piece_width(s, lax.rem(step, SPLIT)), widths, wait)
            return 0

        lax.fori_loop(1, parts, one, 0)

    def result_copies(step, act_remote, act_local):
        c, d, k, piece = pair(q, step)
        slot = lax.rem(step, OUT_SLOTS)

        def one(i, _):
            who = lax.rem(q + i, parts)
            sized(piece_width(s, piece), widths, functools.partial(send_block, who))
            return 0

        def send_block(who, w):
            cols = pl.ds(pl.multiple_of(piece * width, width), w)
            src = obuf.at[slot, pl.ds(who * block, block), pl.ds(0, w)]
            dst = out_ref.at[c, s * per + k, :, cols]
            here = (d == s) & (who == q)

            @pl.when(here)
            def _():
                act_local(pltpu.make_async_copy(src, dst, osend_sem.at[slot, who]))

            @pl.when(jnp.logical_not(here))
            def _():
                act_remote(
                    pltpu.make_async_remote_copy(
                        src_ref=src,
                        dst_ref=dst,
                        send_sem=osend_sem.at[slot, who],
                        recv_sem=orecv_sem.at[c, s * per + k],
                        device_id={"rad": who, "mode": d},
                        device_id_type=pl.DeviceIdType.MESH,
                    )
                )

        lax.fori_loop(0, parts, one, 0)

    zero_pad = jnp.zeros((PAD, width), jnp.bfloat16)

    def clear(step, _):
        recv[step, pl.ds(0, PAD), :] = zero_pad
        recv[step, pl.ds(PAD + shells, PAD), :] = zero_pad

        def clear_dead(w):
            if w < width:
                recv[step, pl.ds(PAD, shells), pl.ds(w, width - w)] = jnp.zeros(
                    (shells, width - w), jnp.bfloat16
                )

        sized(piece_width(s, lax.rem(step, SPLIT)), widths, clear_dead)
        return 0

    def fill(i, act):
        c = i // rows
        row = lax.rem(i, rows)

        def one(w):
            if w < slots:
                act(
                    pltpu.make_async_copy(
                        zeros.at[:, pl.ds(0, slots - w)],
                        out_ref.at[c, row, :, pl.ds(w, slots - w)],
                        fill_sem.at[c, row],
                    )
                )

        sized(live_width(row // per), wholes, one)
        return 0

    zeros[...] = jnp.zeros_like(zeros)
    lax.fori_loop(0, 2 * rows, lambda i, _: fill(i, lambda r: r.start()), 0)
    lax.fori_loop(0, steps, clear, 0)
    load.wait()
    pl.semaphore_wait(barrier, count - 1)
    for first in range(AHEAD):
        push(jnp.int32(first))

    load_basis.wait()
    load_dual.wait()

    def add_identity(i, _):
        at = pl.ds(pl.multiple_of(i * ROWS, ROWS), ROWS)
        row = lax.broadcasted_iota(jnp.int32, (ROWS, shells), 0) + i * ROWS
        col = lax.broadcasted_iota(jnp.int32, (ROWS, shells), 1)
        eye = jnp.where(row == col, 1.0, 0.0).astype(jnp.float32)
        basis[at, :] = (eye + basis[at, :].astype(jnp.float32)).astype(jnp.bfloat16)
        dual[at, :] = (eye + dual[at, :].astype(jnp.float32)).astype(jnp.bfloat16)
        return 0

    lax.fori_loop(0, shells // ROWS, add_identity, 0)

    def body(step, _):
        @pl.when(step + AHEAD < steps)
        def _():
            push(step + AHEAD)

        arrive(step)
        c, d, k, piece = pair(q, step)
        row_id = order_ref[d * rows + s * per + k]
        limit = count_ref[row_id]
        order = (row_id * slots) // (2 * orders)
        slot = lax.rem(step, OUT_SLOTS)

        def table(ct):
            ids = (
                lax.broadcasted_iota(jnp.int32, (1, TILE), 1) + piece * width + ct * TILE
            )
            degree = (order + ids).astype(jnp.float32)
            return degree * (degree + 1.0), ids < limit

        def stencil(i, _):
            ct = lax.rem(i, width // TILE)
            rb = i // (width // TILE)
            at = pl.multiple_of(rb * ROWS, ROWS)
            cols = pl.ds(pl.multiple_of(ct * TILE, TILE), TILE)
            ext = recv[step, pl.ds(at, ROWS + 2 * PAD), cols].astype(jnp.float32)
            size = ROWS + 2 * PAD

            def near(o):
                return pltpu.roll(ext, (size - o) % size, 0)[PAD : PAD + ROWS]

            f = ext[PAD : PAD + ROWS]
            second = (
                16.0 * (near(-1) + near(1)) - (near(-2) + near(2)) - 30.0 * f
            ) * (1.0 / 12.0)
            ll, live = table(ct)
            shell = lax.broadcasted_iota(jnp.int32, (ROWS, 1), 0) + at
            rho = 1.2 + shell.astype(jnp.float32) / shells
            inverse = 1.0 / ((shells * rho) * (shells * rho))
            half = 0.5 * kappa_ref[pl.ds(at, ROWS), :]
            value = f + half * (second - (ll * inverse) * f)
            value = jnp.where(live, value, 0.0)
            upd[pl.ds(at, ROWS), cols] = value.astype(jnp.bfloat16)
            return 0

        lax.fori_loop(0, (shells // ROWS) * (width // TILE), stencil, 0)

        @pl.when(step >= OUT_SLOTS)
        def _():
            result_copies(
                step - OUT_SLOTS, lambda r: r.wait_send(), lambda l: l.wait()
            )

        def transform(ct, _):
            cols = pl.ds(pl.multiple_of(ct * TILE, TILE), TILE)
            ll, live = table(ct)
            projected = jnp.dot(
                dual[...], upd[:, cols], preferred_element_type=jnp.float32
            )
            divisor = eigen_ref[...] + ll * (0.5 / (slots * slots))
            scaled = (projected / divisor).astype(jnp.bfloat16)
            restored = jnp.dot(basis[...], scaled, preferred_element_type=jnp.float32)
            obuf[slot, :, cols] = jnp.where(live, restored, 0.0).astype(jnp.bfloat16)
            return 0

        lax.fori_loop(0, width // TILE, transform, 0)
        result_copies(step, lambda r: r.start(), lambda l: l.start())
        return 0

    lax.fori_loop(0, steps, body, 0)

    def drain_send(i, _):
        step = steps - SEND_SLOTS + i // (parts - 1)
        who = lax.rem(q + 1 + lax.rem(i, parts - 1), parts)
        shell_copy(who, step, lambda r: r.wait_send())
        return 0

    lax.fori_loop(0, SEND_SLOTS * (parts - 1), drain_send, 0)

    def drain_out(i, _):
        result_copies(
            steps - OUT_SLOTS + i, lambda r: r.wait_send(), lambda l: l.wait()
        )
        return 0

    lax.fori_loop(0, OUT_SLOTS, drain_out, 0)

    def landed(i, _):
        c = i // rows
        row = lax.rem(i, rows)
        source = row // per
        p = s * per + lax.rem(row, per)
        who = 2 * c + lax.rem(p, 2)

        def wait(w):
            pltpu.make_async_remote_copy(
                src_ref=out_ref.at[c, row, :, pl.ds(0, w)],
                dst_ref=out_ref.at[c, row, :, pl.ds(0, w)],
                send_sem=osend_sem.at[0, 0],
                recv_sem=orecv_sem.at[c, row],
                device_id={"rad": who, "mode": source},
                device_id_type=pl.DeviceIdType.MESH,
            ).wait_recv()

        @pl.when(jnp.logical_not((source == s) & (who == q)))
        def _():
            sized(live_width(source), wholes, wait)

        return 0

    lax.fori_loop(0, 2 * rows, lambda i, _: fill(i, lambda r: r.wait()), 0)
    lax.fori_loop(0, 2 * rows, landed, 0)


def on_device(
    spectra, diffusivity, eigenvalues, radial_basis, dual_basis, degree_count, order_slot
):
    _, rows, block, slots = spectra.shape
    shells = diffusivity.shape[0]
    orders = degree_count.shape[0]
    parts = lax.axis_size("rad")
    modes = lax.axis_size("mode")
    steps = 2 * rows // parts * SPLIT
    width = slots // SPLIT
    bf16 = jnp.bfloat16
    dma = pltpu.SemaphoreType.DMA
    sizes = (parts, modes, rows, shells, slots, orders)
    vmem = pl.BlockSpec(memory_space=pltpu.VMEM)
    smem = pl.BlockSpec(memory_space=pltpu.SMEM)
    hbm = pl.BlockSpec(memory_space=pl.ANY)
    return pl.pallas_call(
        functools.partial(kernel, sizes),
        out_shape=jax.ShapeDtypeStruct(spectra.shape, bf16),
        in_specs=[smem, smem, hbm, vmem, vmem, hbm, hbm],
        out_specs=hbm,
        scratch_shapes=[
            pltpu.VMEM(spectra.shape, bf16),
            pltpu.VMEM((shells, shells), bf16),
            pltpu.VMEM((shells, shells), bf16),
            pltpu.VMEM((steps, shells + 2 * PAD, width), bf16),
            pltpu.VMEM((SEND_SLOTS, parts, block, width), bf16),
            pltpu.VMEM((shells, width), bf16),
            pltpu.VMEM((OUT_SLOTS, shells, width), bf16),
            pltpu.VMEM((block, slots // 2), bf16),
            dma((3,)),
            dma((SEND_SLOTS, parts)),
            dma((steps, parts)),
            dma((OUT_SLOTS, parts)),
            dma((2, rows)),
            dma((2, rows)),
        ],
        compiler_params=pltpu.CompilerParams(
            collective_id=0,
            has_side_effects=True,
            vmem_limit_bytes=60 * 1024 * 1024,
        ),
    )(
        order_slot,
        degree_count,
        spectra,
        diffusivity.reshape(shells, 1),
        eigenvalues.reshape(shells, 1),
        radial_basis,
        dual_basis,
    )


def solution(mesh):
    placed = (P(None, "mode", "rad", None), P(), P(), P(), P(), P(), P())
    return jax.shard_map(
        on_device,
        mesh=mesh,
        in_specs=placed,
        out_specs=P(None, "mode", "rad", None),
        check_vma=False,
    )
```
